256 devices in a mesh: ev: 32 (over y, z_lo, core), st: 8 (over z_hi, x).
Axes of the slice: x: 4, y: 4, z: 8 (z_hi: 2, z_lo: 4; z = z_hi * 4 + z_lo), core: 2. Of those that a mesh axis runs over, the one named last changes fastest.
Arguments:
- strain: bfloat16 [2, 6, 512, 8192], P(None, None, 'ev'), may hold values from -0.048339844 to 0.048339844
- green: bfloat16 [2, 3, 1024, 6, 8192], P(None, None, 'st', None, 'ev'), may hold values from -6 to 6
- weights: bfloat16 [2, 3, 512, 1024], P(None, None, 'ev', 'st'), may hold values from -0.078125 to 0.078125
- mask: int32 [512, 1024], P('ev', 'st'), may hold values 0 or 1
Outputs:
- kernels: float32 [2, 8192], P(None, ('ev', 'st'))
The draws below stay inside these ranges and needn't reach their ends.
All inputs are finite; a program needn't handle non-finite values. No bound on the sum of `mask` on one device may be relied on, other than what follows from the above.
Results may differ from the reference program's by a relative error of at most 0.0003.
Values may be sent and summed in bfloat16 or wider, within the bound.
A program may use at most 128 MiB of HBM per device.

```python
import jax
import jax.numpy as jnp
from jax import lax

XI = 256
EV = 512
ST = 1024
X = 8192


def set_ends(values, key, least, high):
    longest = values.shape.index(max(values.shape))
    spots = []
    for shift in (0, 1):
        where = [jax.random.randint(jax.random.fold_in(key, axis), (), 0, length) for axis, length in enumerate(values.shape)]
        where[longest] = (where[longest] + shift) % values.shape[longest]
        spots.append(tuple(where))
    return values.at[spots[0]].set(least).at[spots[1]].set(high)


def strengthened(entries, rng, source, target, shards_of, factor):
    def block_of(position):
        return (jnp.arange(entries.shape[position]) // (entries.shape[position] // shards_of)).reshape((-1,) + (1,) * (entries.ndim - 1 - position))

    one_side = jax.random.permutation(rng, shards_of)[block_of(target)]
    other_side = (block_of(target) + shards_of // 2) % shards_of
    return jnp.where((block_of(source) == one_side) | (block_of(source) == other_side), factor * entries, entries)


def levels(rng, dims, cuts, low, largest):
    gain = 1.0
    for dim, parts in cuts:
        draws = jax.random.uniform(jax.random.fold_in(jax.random.fold_in(rng, 6), dim), (parts,), jnp.float32, low / len(cuts), largest / len(cuts))
        gain = gain * jnp.repeat(jnp.exp(draws), dims[dim] // parts).reshape((-1,) + (1,) * (len(dims) - 1 - dim))
    return gain


def bell_draw(key, dims, width, limit, shards=(), held_as=jnp.bfloat16):
    loudness = levels(key, dims, shards, -0.22, 0.18) if shards else 1.0
    values = jax.random.normal(key, dims, jnp.float32) * width * loudness
    return jnp.minimum(jnp.maximum(values, -limit), limit).astype(held_as)


def heavy_noise(own_key, dims, spread, most, shards, heavy, kind=jnp.bfloat16):
    result = spread * jax.random.normal(own_key, dims, jnp.float32)
    if shards:
        result = result * levels(own_key, dims, shards, -0.22, 0.18)
    return jnp.clip(strengthened(result, jax.random.fold_in(own_key, 3), *heavy), -most, most).astype(kind)


def setup_inputs(seed: int = 0) -> dict:
    keys = jax.random.split(jax.random.key(seed), 5)
    return {
        "strain": bell_draw(keys[0], (2, 6, EV, X), (1.0 / (30 * EV) ** 0.5), 0.048339844, ((2, 32),)),
        "green": heavy_noise(keys[1], (2, 3, ST, 6, X), 1.0, 6.0, ((2, 8), (4, 32)), (2, 4, 32, 2.75)),
        "weights": bell_draw(keys[2], (2, 3, EV, ST), (6 * ST) ** -0.5, 0.078125, ((2, 32), (3, 8))),
        "mask": set_ends((jax.random.randint(keys[3], (EV, ST), 0, 4) < 3).astype(jnp.int32), jax.random.fold_in(keys[3], 1), 0, 1),
    }


def reference(strain, green, weights, mask):
    weighted = (weights * mask.astype(jnp.bfloat16)[None, None]).astype(jnp.float32)
    voigt = jnp.array([1.0, 1.0, 1.0, 2.0, 2.0, 2.0], jnp.float32)

    def one_block(block_index):
        first_cell = (block_index * XI).astype(jnp.int32)
        green_block = lax.dynamic_slice_in_dim(green, first_cell, XI, 4).astype(jnp.float32)
        strain_block = lax.dynamic_slice_in_dim(strain, first_cell, XI, 3).astype(jnp.float32)
        products = jnp.einsum("rfes,qfscx->rqecx", weighted, green_block, precision=lax.Precision.HIGHEST)
        held_real = products[0, 0] - products[1, 1]
        held_imag = products[0, 1] + products[1, 0]
        strain_real = jnp.swapaxes(strain_block[0], 0, 1)
        strain_imag = jnp.swapaxes(strain_block[1], 0, 1)
        trace_term = jnp.sum(strain_real[:, :3].sum(1) * held_real[:, :3].sum(1) - strain_imag[:, :3].sum(1) * held_imag[:, :3].sum(1), axis=0)
        shear_term = jnp.sum((strain_real * held_real - strain_imag * held_imag) * voigt[None, :, None], axis=(0, 1))
        return jnp.stack([trace_term, shear_term])

    blocks = lax.map(one_block, jnp.arange(X // XI, dtype=jnp.int32))
    return jnp.transpose(blocks, (1, 0, 2)).reshape(2, X)
```

```python
import jax
import jax.numpy as jnp
from jax import lax
from jax.experimental import pallas as pl
from jax.experimental.pallas import tpu as pltpu
from jax.sharding import PartitionSpec as P

MESH = pl.DeviceIdType.MESH
OFF_AXIS = (1, 3, 2)
GROUPS = tuple((dc, dy) for dy in OFF_AXIS for dc in (0, 1))


def kernel(strain, green, weights, mask, out, sbuf, wbuf, gs, lhs, held, acc, kbuf, krx,
           lsem, ssem, r_s, r_x, r_wz, r_wy, r_wc, r_k):
    ev, st = lax.axis_index("ev"), lax.axis_index("st")
    y, zl, c = ev // 8, (ev // 2) % 4, ev % 2
    zh, x = st // 4, st % 4
    z = zh * 4 + zl

    def device(x_, y_, z_, c_):
        x_, y_, z_ = (x_ + 4) % 4, (y_ + 4) % 4, (z_ + 8) % 8
        return ((y_ * 4 + z_ % 4) * 2 + c_, (z_ // 4) * 4 + x_)

    def far(dz, core):
        return {0: 0, 1: 1, 3: -1}[dz] if dz != 2 else 2 - 4 * core

    def in_half(dz):
        return zh * 4 + (zl + dz) % 4

    sends = []

    def send(src, dst, recv_sem, to):
        copy = pltpu.make_async_remote_copy(
            src_ref=src, dst_ref=dst, send_sem=ssem.at[len(sends)], recv_sem=recv_sem,
            device_id=to, device_id_type=MESH)
        copy.start()
        sends.append(copy)
        return copy

    load_green = [
        pltpu.make_async_copy(green.at[k], gs.at[:, pl.ds(k * 128, 128), :], lsem.at[1 + k]) for k in range(6)]
    for copy in load_green:
        copy.start()

    def cells(ev_):
        return pl.ds(pl.multiple_of(ev_ * 256, 256), 256)

    load_own = pltpu.make_async_copy(strain.at[:, :, cells(ev)], sbuf.at[0, 0, 0], lsem.at[0])
    load_own.start()

    barrier = pltpu.get_barrier_semaphore()
    senders = [device(x, y, z, 1 - c)]
    for dy in range(4):
        for dz in range(4):
            if dy or dz:
                for core in (0, 1):
                    senders.append(device(x, y - dy, z - far(dz, c), core))
    for dz in (1, 2, 3):
        senders.append(device(x, y, in_half(4 - dz), c))
    for dx in range(4):
        for dh in (0, 4):
            if dx or dh:
                senders.append(device(x + dx, y, z + dh, c))
    for d in senders:
        pl.semaphore_signal(barrier, inc=1, device_id=d, device_id_type=MESH)
    wbuf[0, 0, 0] = weights[...] * mask[...].astype(jnp.bfloat16)[None]
    pl.semaphore_wait(barrier, len(senders))

    wz = [send(wbuf.at[0, 0, 0], wbuf.at[0, 0, dz], r_wz.at[dz], device(x, y, in_half(dz), c)) for dz in (1, 2, 3)]

    mine = pl.ds(3 * x, 3)
    def strain_to(dy, dz, dc, slabs):
        core = c if dc == 0 else 1 - c
        to = device(x, y + dy, z + far(dz, core), core)
        return send(strain.at[slabs, :, cells(to[0])], sbuf.at[dc, dy, dz, slabs], r_s.at[dc, dy, dz], to)

    quarters = {}
    for dc, dy in GROUPS:
        quarters[dc, dy] = [strain_to(dy, dz, dc, mine) for dz in (1, 2, 3)]
    whole = pl.ds(0, 12)
    direct = [strain_to(0, 0, 1, whole)]
    for dy, dz in ((1, 0), (0, 1), (3, 0), (0, 3), (2, 0), (0, 2)):
        for dc in (0, 1):
            direct.append(strain_to(dy, dz, dc, whole))

    for copy in wz:
        copy.wait_recv()
    wy = [send(wbuf.at[0, 0], wbuf.at[0, dy], r_wy.at[dy], device(x, y + dy, z, c)) for dy in (1, 3, 2)]

    right, left = device(x + 1, y, z, c), device(x - 1, y, z, c)

    def part(dc, dy, of_x):
        return sbuf.at[dc, dy, pl.ds(1, 3), pl.ds(3 * ((of_x + 4) % 4), 3)]

    to_right, to_left, relays = {}, {}, {}
    for g, (dc, dy) in enumerate(GROUPS):
        for copy in quarters[dc, dy]:
            copy.wait_recv()
        p = part(dc, dy, x)
        to_right[g] = send(p, p, r_x.at[0, g], right)
        to_left[g] = send(p, p, r_x.at[1, g], left)

    for copy in wy:
        copy.wait_recv()
    wc = send(wbuf.at[0], wbuf.at[1], r_wc.at[0], device(x, y, z, 1 - c))

    def relay(g):
        dc, dy = GROUPS[g]
        if dc == 0:
            to_right[g].wait_recv()
            p = part(dc, dy, x - 1)
            relays[g] = send(p, p, r_x.at[2, g], right)
        else:
            to_left[g].wait_recv()
            p = part(dc, dy, x + 1)
            relays[g] = send(p, p, r_x.at[2, g], left)

    relay(0)
    relay(1)
    wc.wait_recv()
    all_w = wbuf.reshape(32, 6, 16, 128)
    for f in range(3):
        real = all_w[:, f].reshape(512, 128)
        imag = all_w[:, 3 + f].reshape(512, 128)
        lhs[0:512, f * 128:(f + 1) * 128] = real
        lhs[0:512, 384 + f * 128:384 + (f + 1) * 128] = -imag
        lhs[512:1024, f * 128:(f + 1) * 128] = imag
        lhs[512:1024, 384 + f * 128:384 + (f + 1) * 128] = real

    def multiply(v, _):
        held[v] = jnp.dot(lhs[...], gs[v], preferred_element_type=jnp.float32)
        return 0

    for copy in load_green:
        copy.wait()
    lax.fori_loop(0, 3, multiply, 0)
    relay(2)
    relay(3)
    lax.fori_loop(3, 6, multiply, 0)
    relay(4)
    relay(5)

    acc[...] = jnp.zeros_like(acc)

    def add_up(slot):
        dc, dy, dz = slot
        row = (dc * 16 + dy * 4 + dz) * 16
        s = sbuf[dc, dy, dz].astype(jnp.float32)
        hr = [held[v, pl.ds(row, 16), :] for v in range(6)]
        hi = [held[v, pl.ds(512 + row, 16), :] for v in range(6)]
        trace = (s[0] + s[1] + s[2]) * (hr[0] + hr[1] + hr[2]) - (s[6] + s[7] + s[8]) * (hi[0] + hi[1] + hi[2])
        normal = sum(s[v] * hr[v] - s[6 + v] * hi[v] for v in range(3))
        shear = sum(s[v] * hr[v] - s[6 + v] * hi[v] for v in range(3, 6))
        acc[0] += trace
        acc[1] += normal + 2.0 * shear

    load_own.wait()
    add_up((0, 0, 0))
    for copy in direct:
        copy.wait_recv()
    add_up((1, 0, 0))
    for dy, dz in ((1, 0), (0, 1), (3, 0), (0, 3), (2, 0), (0, 2)):
        for dc in (0, 1):
            add_up((dc, dy, dz))
    for g, (dc, dy) in enumerate(GROUPS):
        if dc == 0:
            to_left[g].wait_recv()
        else:
            to_right[g].wait_recv()
        relays[g].wait_recv()
        for dz in (1, 2, 3):
            add_up((dc, dy, dz))

    total = acc[...].sum(axis=1)
    kbuf[0, 0:2] = total[:, 0:128]
    kbuf[1, 0:2] = total[:, 128:256]
    shares = []
    for dx in range(4):
        for dh in (0, 1):
            if dx or dh:
                h = (zh + dh) % 2
                shares.append(send(kbuf.at[h], krx.at[dx * 2 + dh], r_k.at[dx * 2 + dh],
                                   device(x + dx, y, h * 4 + zl, c)))
    own = kbuf[zh]
    for copy in shares:
        copy.wait_recv()
    for k in range(1, 8):
        own = own + krx[k]
    own = own[0:2]
    result = own[:, 0:32]
    for k in range(1, 4):
        result = jnp.where(x == k, own[:, 32 * k:32 * k + 32], result)
    out[...] = result
    for copy in sends:
        copy.wait_send()


def local(strain, green, weights, mask):
    return pl.pallas_call(
        kernel,
        out_shape=jax.ShapeDtypeStruct((2, 32), jnp.float32),
        in_specs=[
            pl.BlockSpec(memory_space=pl.ANY),
            pl.BlockSpec(memory_space=pl.ANY),
            pl.BlockSpec(memory_space=pltpu.VMEM),
            pl.BlockSpec(memory_space=pltpu.VMEM),
        ],
        out_specs=pl.BlockSpec(memory_space=pltpu.VMEM),
        scratch_shapes=[
            pltpu.VMEM((2, 4, 4, 12, 16, 256), jnp.bfloat16),
            pltpu.VMEM((2, 4, 4, 6, 16, 128), jnp.bfloat16),
            pltpu.VMEM((6, 768, 256), jnp.bfloat16),
            pltpu.VMEM((1024, 768), jnp.bfloat16),
            pltpu.VMEM((6, 1024, 256), jnp.float32),
            pltpu.VMEM((2, 16, 256), jnp.float32),
            pltpu.VMEM((2, 8, 128), jnp.float32),
            pltpu.VMEM((8, 8, 128), jnp.float32),
            pltpu.SemaphoreType.DMA((7,)),
            pltpu.SemaphoreType.DMA((64,)),
            pltpu.SemaphoreType.DMA((2, 4, 4)),
            pltpu.SemaphoreType.DMA((3, 6)),
            pltpu.SemaphoreType.DMA((4,)),
            pltpu.SemaphoreType.DMA((4,)),
            pltpu.SemaphoreType.DMA((1,)),
            pltpu.SemaphoreType.DMA((8,)),
        ],
        compiler_params=pltpu.CompilerParams(
            collective_id=0, has_side_effects=True, vmem_limit_bytes=60 << 20),
    )(strain.reshape(12, *strain.shape[2:]), jnp.swapaxes(green, 2, 3).reshape(6, 6, 128, 256),
      weights.reshape(6, *weights.shape[2:]), mask)


def solution(mesh):
    return jax.shard_map(
        local,
        mesh=mesh,
        in_specs=(
            P(None, None, "ev", None),
            P(None, None, "st", None, "ev"),
            P(None, None, "ev", "st"),
            P("ev", "st"),
        ),
        out_specs=P(None, ("ev", "st")),
        check_vma=False,
    )
```

```python
import jax
import jax.numpy as jnp
from jax import lax
from jax.experimental import pallas as pl
from jax.experimental.pallas import tpu as pltpu
from jax.sharding import PartitionSpec as P

MESH = pl.DeviceIdType.MESH
CORNERS = ((1, 1), (3, 3), (1, 3), (3, 1), (1, 2), (2, 1), (3, 2), (2, 3), (2, 2))
ALONG = ((1, 0), (0, 1), (3, 0), (0, 3), (2, 0), (0, 2))


def kernel(strain, green, weights, mask, out, sbuf, wbuf, gs, lhs, held, acc, kbuf, krx,
           lsem, ssem, r_s, r_x, r_wz, r_wy, r_wc, r_k):
    ev, st = lax.axis_index("ev"), lax.axis_index("st")
    y, zl, c = ev // 8, (ev // 2) % 4, ev % 2
    zh, x = st // 4, st % 4
    z = zh * 4 + zl

    def device(x_, y_, z_, c_):
        x_, y_, z_ = (x_ + 4) % 4, (y_ + 4) % 4, (z_ + 8) % 8
        return ((y_ * 4 + z_ % 4) * 2 + c_, (z_ // 4) * 4 + x_)

    def far(dz, core):
        return {0: 0, 1: 1, 3: -1}[dz] if dz != 2 else 2 - 4 * core

    def in_half(dz):
        return zh * 4 + (zl + dz) % 4

    sends = []

    def send(src, dst, recv_sem, to):
        copy = pltpu.make_async_remote_copy(
            src_ref=src, dst_ref=dst, send_sem=ssem.at[len(sends)], recv_sem=recv_sem,
            device_id=to, device_id_type=MESH)
        copy.start()
        sends.append(copy)
        return copy

    load_green = [
        pltpu.make_async_copy(green.at[k], gs.at[:, pl.ds(k * 128, 128), :], lsem.at[1 + k]) for k in range(6)]
    for copy in load_green:
        copy.start()

    def cells(ev_):
        return pl.ds(pl.multiple_of(ev_ * 256, 256), 256)

    load_own = pltpu.make_async_copy(strain.at[:, :, cells(ev)], sbuf.at[0, 0, 0], lsem.at[0])
    load_own.start()

    barrier = pltpu.get_barrier_semaphore()
    senders = [device(x, y, z, 1 - c)]
    for dy in (2, 1, 3, 0):
        for dz in (2, 1, 3, 0):
            if dy or dz:
                for core in (0, 1):
                    senders.append(device(x, y - dy, z - far(dz, c), core))
    for dz in (1, 2, 3):
        senders.append(device(x, y, in_half(4 - dz), c))
    for dx in (1, 3):
        senders.append(device(x + dx, y, z, c))
    for d in senders:
        pl.semaphore_signal(barrier, inc=1, device_id=d, device_id_type=MESH)
    wbuf[0, 0, 0] = weights[...] * mask[...].astype(jnp.bfloat16)[None]
    pl.semaphore_wait(barrier, len(senders))

    wz = [send(wbuf.at[0, 0, 0], wbuf.at[0, 0, dz], r_wz.at[dz], device(x, y, in_half(dz), c)) for dz in (1, 2, 3)]

    mine = pl.ds(3 * x, 3)
    def strain_to(dy, dz, dc, slabs):
        core = c if dc == 0 else 1 - c
        to = device(x, y + dy, z + far(dz, core), core)
        return send(strain.at[slabs, :, cells(to[0])], sbuf.at[dc, dy, dz, slabs], r_s.at[dc, dy, dz], to)

    corner = {}
    for dy, dz in CORNERS:
        corner[dy, dz] = [strain_to(dy, dz, dc, mine) for dc in (0, 1)]
    whole = pl.ds(0, 12)

    for copy in wz:
        copy.wait_recv()
    wy = [send(wbuf.at[0, 0], wbuf.at[0, dy], r_wy.at[dy], device(x, y + dy, z, c)) for dy in (1, 3, 2)]
    direct = [strain_to(dy, dz, dc, whole) for dy, dz in ALONG for dc in (0, 1)]
    direct.append(strain_to(0, 0, 1, whole))

    right, left = device(x + 1, y, z, c), device(x - 1, y, z, c)

    def part(dcs, g, of_x):
        return sbuf.at[dcs, CORNERS[g][0], CORNERS[g][1], pl.ds(3 * ((of_x + 4) % 4), 3)]

    to_right, to_left, relay_right, relay_left = {}, {}, {}, {}
    both = pl.ds(0, 2)

    def forward(g):
        for copy in corner[CORNERS[g]]:
            copy.wait_recv()
        p = part(both, g, x)
        to_right[g] = send(p, p, r_x.at[0, g], right)
        to_left[g] = send(p, p, r_x.at[1, g], left)

    def relay(g):
        to_right[g].wait_recv()
        p = part(0, g, x - 1)
        relay_right[g] = send(p, p, r_x.at[2, g], right)
        to_left[g].wait_recv()
        p = part(1, g, x + 1)
        relay_left[g] = send(p, p, r_x.at[3, g], left)

    def middle_weights():
        for copy in wy:
            copy.wait_recv()
        sib.append(send(wbuf.at[0], wbuf.at[1], r_wc.at[0], device(x, y, z, 1 - c)))

    sib = []

    def left_side():
        sib[0].wait_recv()
        all_w = wbuf.reshape(32, 6, 16, 128)
        for f in range(3):
            real = all_w[:, f].reshape(512, 128)
            imag = all_w[:, 3 + f].reshape(512, 128)
            lhs[0:512, f * 128:(f + 1) * 128] = real
            lhs[0:512, 384 + f * 128:384 + (f + 1) * 128] = -imag
            lhs[512:1024, f * 128:(f + 1) * 128] = imag
            lhs[512:1024, 384 + f * 128:384 + (f + 1) * 128] = real
        for copy in load_green:
            copy.wait()

    def multiply(v, _):
        held[v] = jnp.dot(lhs[...], gs[v], preferred_element_type=jnp.float32)
        return 0

    def products(first, last):
        lax.fori_loop(first, last, multiply, 0)

    forward(0)
    forward(1)
    forward(2)
    forward(3)
    relay(0)
    relay(1)
    forward(4)
    forward(5)
    relay(2)
    relay(3)
    forward(6)
    forward(7)
    relay(4)
    relay(5)
    middle_weights()
    forward(8)
    relay(6)
    left_side()
    products(0, 2)
    relay(7)
    products(2, 4)
    relay(8)
    products(4, 6)

    acc[...] = jnp.zeros_like(acc)

    def add_up(slot):
        dc, dy, dz = slot
        row = (dc * 16 + dy * 4 + dz) * 16
        s = sbuf[dc, dy, dz].astype(jnp.float32)
        hr = [held[v, pl.ds(row, 16), :] for v in range(6)]
        hi = [held[v, pl.ds(512 + row, 16), :] for v in range(6)]
        trace = (s[0] + s[1] + s[2]) * (hr[0] + hr[1] + hr[2]) - (s[6] + s[7] + s[8]) * (hi[0] + hi[1] + hi[2])
        normal = sum(s[v] * hr[v] - s[6 + v] * hi[v] for v in range(3))
        shear = sum(s[v] * hr[v] - s[6 + v] * hi[v] for v in range(3, 6))
        acc[0] += trace
        acc[1] += normal + 2.0 * shear

    load_own.wait()
    add_up((0, 0, 0))
    for copy in direct:
        copy.wait_recv()
    add_up((1, 0, 0))
    for dy, dz in ALONG:
        for dc in (0, 1):
            add_up((dc, dy, dz))
    for copy in sends:
        copy.wait_send()
    done = len(sends)
    for g, (dy, dz) in enumerate(CORNERS):
        relay_right[g].wait_recv()
        relay_left[g].wait_recv()
        for dc in (0, 1):
            add_up((dc, dy, dz))

    total = acc[...].sum(axis=1)
    kbuf[0, 0:2] = total[:, 0:128]
    kbuf[1, 0:2] = total[:, 128:256]
    shares = []
    for dx in range(4):
        for dh in (0, 1):
            if dx or dh:
                h = (zh + dh) % 2
                shares.append(send(kbuf.at[h], krx.at[dx * 2 + dh], r_k.at[dx * 2 + dh],
                                   device(x + dx, y, h * 4 + zl, c)))
    own = kbuf[zh]
    for copy in shares:
        copy.wait_recv()
    for k in range(1, 8):
        own = own + krx[k]
    own = own[0:2]
    result = own[:, 0:32]
    for k in range(1, 4):
        result = jnp.where(x == k, own[:, 32 * k:32 * k + 32], result)
    out[...] = result
    for copy in sends[done:]:
        copy.wait_send()


def local(strain, green, weights, mask):
    return pl.pallas_call(
        kernel,
        out_shape=jax.ShapeDtypeStruct((2, 32), jnp.float32),
        in_specs=[
            pl.BlockSpec(memory_space=pl.ANY),
            pl.BlockSpec(memory_space=pl.ANY),
            pl.BlockSpec(memory_space=pltpu.VMEM),
            pl.BlockSpec(memory_space=pltpu.VMEM),
        ],
        out_specs=pl.BlockSpec(memory_space=pltpu.VMEM),
        scratch_shapes=[
            pltpu.VMEM((2, 4, 4, 12, 16, 256), jnp.bfloat16),
            pltpu.VMEM((2, 4, 4, 6, 16, 128), jnp.bfloat16),
            pltpu.VMEM((6, 768, 256), jnp.bfloat16),
            pltpu.VMEM((1024, 768), jnp.bfloat16),
            pltpu.VMEM((6, 1024, 256), jnp.float32),
            pltpu.VMEM((2, 16, 256), jnp.float32),
            pltpu.VMEM((2, 8, 128), jnp.float32),
            pltpu.VMEM((8, 8, 128), jnp.float32),
            pltpu.SemaphoreType.DMA((7,)),
            pltpu.SemaphoreType.DMA((88,)),
            pltpu.SemaphoreType.DMA((2, 4, 4)),
            pltpu.SemaphoreType.DMA((4, 9)),
            pltpu.SemaphoreType.DMA((4,)),
            pltpu.SemaphoreType.DMA((4,)),
            pltpu.SemaphoreType.DMA((1,)),
            pltpu.SemaphoreType.DMA((8,)),
        ],
        compiler_params=pltpu.CompilerParams(
            collective_id=0, has_side_effects=True, vmem_limit_bytes=60 << 20),
    )(strain.reshape(12, *strain.shape[2:]), jnp.swapaxes(green, 2, 3).reshape(6, 6, 128, 256),
      weights.reshape(6, *weights.shape[2:]), mask)


def solution(mesh):
    return jax.shard_map(
        local,
        mesh=mesh,
        in_specs=(
            P(None, None, "ev", None),
            P(None, None, "st", None, "ev"),
            P(None, None, "ev", "st"),
            P("ev", "st"),
        ),
        out_specs=P(None, ("ev", "st")),
        check_vma=False,
    )
```

```python
import jax
import jax.numpy as jnp
from jax import lax
from jax.experimental import pallas as pl
from jax.experimental.pallas import tpu as pltpu
from jax.sharding import PartitionSpec as P

MESH = pl.DeviceIdType.MESH
CORNERS = ((1, 1), (3, 3), (1, 3), (3, 1), (1, 2), (3, 2), (2, 1), (2, 3), (2, 2))
ALONG = ((1, 0), (0, 1), (3, 0), (0, 3), (2, 0), (0, 2))
FAR, NEAR, WHOLE = 0, 1, 2
WHOLE_GROUPS, WHOLE_ALONG = 6, 4


def kernel(strain, green, weights, mask, out, sbuf, wbuf, gs, lhs, held, acc, kbuf, krx,
           lsem, s_all, r_w, r_c, r_d, r_f, r_r, r_k):
    ev, st = lax.axis_index("ev"), lax.axis_index("st")
    y, zl, c = ev >> 3, (ev >> 1) & 3, ev & 1
    zh, x = st >> 2, st & 3
    z = zh * 4 + zl
    cores = (c, 1 - c)
    row = [((y + dy) & 3) * 8 for dy in range(4)]
    step_z = {(0, k): 0 for k in (0, 1)} | {(1, k): 1 for k in (0, 1)} | {(3, k): -1 for k in (0, 1)}
    step_z |= {(2, k): 2 - 4 * cores[k] for k in (0, 1)}
    place_to = {at: (z + step) & 7 for at, step in step_z.items()}
    place_from = {dz: (z - step_z[dz, 0]) & 7 for dz in range(4)}
    place_half = [zh * 4 + ((zl + dz) & 3) for dz in range(4)]
    xs = [(x + dx) & 3 for dx in range(4)]

    def device(x_, row_, place, core):
        return (row_ + (place & 3) * 2 + core, (place >> 2) * 4 + x_)

    def lanes(part, half):
        if part == WHOLE:
            return pl.ds(0, 256)
        return pl.ds(pl.multiple_of((1 - half if part == FAR else half) * 128, 128), 128)

    def send(src, dst, send_sem, recv_sem, to):
        pltpu.make_async_remote_copy(
            src_ref=src, dst_ref=dst, send_sem=send_sem, recv_sem=recv_sem,
            device_id=to, device_id_type=MESH).start()

    def arrived(ref, sem):
        pltpu.make_async_remote_copy(
            src_ref=ref, dst_ref=ref, send_sem=s_all.at[0], recv_sem=sem,
            device_id=right, device_id_type=MESH).wait_recv()

    def left(ref, sem):
        pltpu.make_async_remote_copy(
            src_ref=ref, dst_ref=ref, send_sem=sem, recv_sem=r_w.at[0],
            device_id=right, device_id_type=MESH).wait_send()

    right_of, left_of = (ev, zh * 4 + xs[1]), (ev, zh * 4 + xs[3])
    right = right_of
    across = (ev + 1 - 2 * c, st)

    barrier = pltpu.get_barrier_semaphore()
    senders = []
    for dy in (2, 1, 3, 0):
        for dz in (2, 1, 3, 0):
            if dy or dz:
                for core in (0, 1):
                    senders.append(device(x, row[-dy], place_from[dz], core))
    for dz in (1, 2, 3):
        senders.append(device(x, row[0], place_half[4 - dz], c))
    for dx in (1, 3):
        senders.append((ev, zh * 4 + xs[dx]))
    senders.append((ev + 1 - 2 * c, st))
    for d in senders:
        pl.semaphore_signal(barrier, inc=1, device_id=d, device_id_type=MESH)

    load_green = [
        pltpu.make_async_copy(green.at[k], gs.at[:, pl.ds(k * 128, 128), :], lsem.at[1 + k]) for k in range(6)]
    for copy in load_green:
        copy.start()
    own_cells = pl.ds(pl.multiple_of(ev * 256, 256), 256)
    load_own = pltpu.make_async_copy(strain.at[:, :, own_cells], sbuf.at[0, 0, 0], lsem.at[0])
    load_own.start()
    wbuf[0, 0, 0] = weights[...] * mask[...].astype(jnp.bfloat16)[None]
    pl.semaphore_wait(barrier, len(senders))

    for dz in (1, 2, 3):
        send(wbuf.at[0, 0, 0], wbuf.at[0, 0, dz], s_all.at[0], r_w.at[0], device(x, row[0], place_half[dz], c))

    mine = pl.ds(3 * x, 3)
    whole = pl.ds(0, 12)
    both = pl.ds(0, 2)

    def strain_to(dy, dz, dc, slabs, part, send_sem, recv_sem):
        place = place_to[dz, dc]
        to = device(x, row[dy], place, cores[dc])
        at = lanes(part, place >> 2)
        start = pl.multiple_of(to[0] * 256 + at.start, 128)
        send(strain.at[slabs, :, pl.ds(start, at.size)], sbuf.at[dc, dy, dz, slabs, :, at], send_sem, recv_sem, to)

    def parts_of(count, first_split):
        for n in range(first_split):
            yield n, WHOLE
        for part in (FAR, NEAR):
            for n in range(first_split, count):
                yield n, part

    GP = list(parts_of(9, WHOLE_GROUPS))
    DP = list(parts_of(6, WHOLE_ALONG))

    def send_corner(g, part):
        for dc in (0, 1):
            strain_to(*CORNERS[g], dc, mine, part, s_all.at[3], r_c.at[g, part])

    def send_direct(n, part):
        for dc in (0, 1):
            strain_to(*ALONG[n], dc, whole, part, s_all.at[4], r_d.at[n, part])

    strain_to(0, 0, 1, whole, WHOLE, s_all.at[5], r_w.at[3])
    for g, part in GP:
        send_corner(g, part)
    arrived(wbuf.at[0, 0, pl.ds(1, 3)], r_w.at[0])
    for dy in (1, 3, 2):
        send(wbuf.at[0, 0], wbuf.at[0, dy], s_all.at[1], r_w.at[1], (row[dy] + (ev & 7), st))
    for n, part in DP:
        send_direct(n, part)

    def block(dcs, g, slabs, part):
        return sbuf.at[dcs, CORNERS[g][0], CORNERS[g][1], slabs, :, lanes(part, zh)]

    def forward(g, part):
        b = block(both, g, mine, part)
        arrived(b, r_c.at[g, part])
        for to in (right_of, left_of):
            send(b, b, s_all.at[6], r_f.at[g, part], to)

    def relay(g, part):
        arrived(block(both, g, pl.ds(0, 6), part), r_f.at[g, part])
        for dc, of_x, to in ((0, xs[3], right_of), (1, xs[1], left_of)):
            b = block(dc, g, pl.ds(3 * of_x, 3), part)
            send(b, b, s_all.at[7], r_r.at[g, part], to)

    def weights_across():
        arrived(wbuf.at[0, pl.ds(1, 3)], r_w.at[1])
        send(wbuf.at[0], wbuf.at[1], s_all.at[2], r_w.at[2], across)

    def left_side():
        arrived(wbuf.at[1], r_w.at[2])
        all_w = wbuf.reshape(32, 6, 16, 128)
        for f in range(3):
            real = all_w[:, f].reshape(512, 128)
            imag = all_w[:, 3 + f].reshape(512, 128)
            lhs[0:512, f * 128:(f + 1) * 128] = real
            lhs[0:512, 384 + f * 128:384 + (f + 1) * 128] = -imag
            lhs[512:1024, f * 128:(f + 1) * 128] = imag
            lhs[512:1024, 384 + f * 128:384 + (f + 1) * 128] = real
        for copy in load_green:
            copy.wait()

    def multiply(v, _):
        held[v] = jnp.dot(lhs[...], gs[v], preferred_element_type=jnp.float32)
        return 0

    def products(first, last):
        lax.fori_loop(first, last, multiply, 0)

    acc[...] = jnp.zeros_like(acc)

    def add_up(slot, part):
        dc, dy, dz = slot
        first = (dc * 16 + dy * 4 + dz) * 16
        at = lanes(part, zh)
        s = sbuf[dc, dy, dz, :, :, at].astype(jnp.float32)
        hr = [held[v, pl.ds(first, 16), at] for v in range(6)]
        hi = [held[v, pl.ds(512 + first, 16), at] for v in range(6)]
        trace = (s[0] + s[1] + s[2]) * (hr[0] + hr[1] + hr[2]) - (s[6] + s[7] + s[8]) * (hi[0] + hi[1] + hi[2])
        normal = sum(s[v] * hr[v] - s[6 + v] * hi[v] for v in range(3))
        shear = sum(s[v] * hr[v] - s[6 + v] * hi[v] for v in range(3, 6))
        acc[0, :, at] += trace
        acc[1, :, at] += normal + 2.0 * shear

    def take_direct(n, part):
        arrived(sbuf.at[both, ALONG[n][0], ALONG[n][1], :, :, lanes(part, zh)], r_d.at[n, part])
        for dc in (0, 1):
            add_up((dc, *ALONG[n]), part)

    def take_corner(g, part):
        arrived(block(both, g, pl.ds(0, 3), part), r_r.at[g, part])
        for dc in (0, 1):
            add_up((dc, *CORNERS[g]), part)

    def share(dh):
        kbuf[dh, 0:2] = acc[:, :, lanes(NEAR if dh == 0 else FAR, zh)].sum(axis=1)
        for dx in (2, 1, 3, 0):
            if dx or dh:
                send(kbuf.at[dh], krx.at[4 * dh + dx], s_all.at[8 + dh], r_k.at[dh], (ev, (zh ^ dh) * 4 + xs[dx]))

    for stage in GP[0:6]:
        forward(*stage)
    for stage in GP[0:2]:
        relay(*stage)
    for stage in GP[6:9]:
        forward(*stage)
    for stage in GP[2:4]:
        relay(*stage)
    for stage in GP[9:12]:
        forward(*stage)
    relay(*GP[4])
    weights_across()
    for stage in GP[5:8]:
        relay(*stage)
    left_side()
    products(0, 3)
    relay(*GP[8])
    products(3, 6)
    for stage in GP[9:12]:
        relay(*stage)
    load_own.wait()
    add_up((0, 0, 0), WHOLE)
    arrived(sbuf.at[1, 0, 0], r_w.at[3])
    add_up((1, 0, 0), WHOLE)
    for stage in DP[0:4]:
        take_direct(*stage)
    for stage in GP[0:6]:
        take_corner(*stage)
    for stage in DP[4:6]:
        take_direct(*stage)
    for stage in GP[6:9]:
        take_corner(*stage)
    share(1)
    for stage in DP[6:8]:
        take_direct(*stage)
    for stage in GP[9:12]:
        take_corner(*stage)
    share(0)
    left(wbuf.at[0, 0, pl.ds(1, 3)], s_all.at[0])
    left(wbuf.at[0, pl.ds(1, 3)], s_all.at[1])
    left(wbuf.at[0], s_all.at[2])
    left(sbuf.at[0, pl.ds(0, 3), pl.ds(0, 3), pl.ds(0, 6)], s_all.at[3])
    left(sbuf.at[0, pl.ds(0, 3)], s_all.at[4])
    left(sbuf.at[0, 0, 0], s_all.at[5])
    left(sbuf.at[0, pl.ds(0, 3), pl.ds(0, 3)], s_all.at[6])
    left(sbuf.at[0, pl.ds(0, 3), pl.ds(0, 3), pl.ds(0, 6)], s_all.at[7])
    arrived(krx.at[pl.ds(4, 4)], r_k.at[1])
    other = krx[4] + krx[5] + krx[6] + krx[7]
    arrived(krx.at[pl.ds(1, 3)], r_k.at[0])
    same = kbuf[0] + krx[1] + krx[2] + krx[3]

    def own_cells_of(total):
        result = total[0:2, 0:32]
        for k in range(1, 4):
            result = jnp.where(x == k, total[0:2, 32 * k:32 * k + 32], result)
        return result

    out[0] = own_cells_of(same)
    out[1] = own_cells_of(other)
    left(krx.at[pl.ds(1, 3)], s_all.at[8])
    left(krx.at[pl.ds(4, 4)], s_all.at[9])


def local(strain, green, weights, mask):
    sums = pl.pallas_call(
        kernel,
        out_shape=jax.ShapeDtypeStruct((2, 2, 32), jnp.float32),
        in_specs=[
            pl.BlockSpec(memory_space=pl.ANY),
            pl.BlockSpec(memory_space=pl.ANY),
            pl.BlockSpec(memory_space=pltpu.VMEM),
            pl.BlockSpec(memory_space=pltpu.VMEM),
        ],
        out_specs=pl.BlockSpec(memory_space=pltpu.VMEM),
        scratch_shapes=[
            pltpu.VMEM((2, 4, 4, 12, 16, 256), jnp.bfloat16),
            pltpu.VMEM((2, 4, 4, 6, 16, 128), jnp.bfloat16),
            pltpu.VMEM((6, 768, 256), jnp.bfloat16),
            pltpu.VMEM((1024, 768), jnp.bfloat16),
            pltpu.VMEM((6, 1024, 256), jnp.float32),
            pltpu.VMEM((2, 16, 256), jnp.float32),
            pltpu.VMEM((2, 8, 128), jnp.float32),
            pltpu.VMEM((8, 8, 128), jnp.float32),
            pltpu.SemaphoreType.DMA((7,)),
            pltpu.SemaphoreType.DMA((10,)),
            pltpu.SemaphoreType.DMA((4,)),
            pltpu.SemaphoreType.DMA((9, 3)),
            pltpu.SemaphoreType.DMA((6, 3)),
            pltpu.SemaphoreType.DMA((9, 3)),
            pltpu.SemaphoreType.DMA((9, 3)),
            pltpu.SemaphoreType.DMA((2,)),
        ],
        compiler_params=pltpu.CompilerParams(
            collective_id=0, has_side_effects=True, vmem_limit_bytes=60 << 20),
    )(strain.reshape(12, *strain.shape[2:]), jnp.swapaxes(green, 2, 3).reshape(6, 6, 128, 256),
      weights.reshape(6, *weights.shape[2:]), mask)
    return sums[0] + sums[1]


def solution(mesh):
    return jax.shard_map(
        local,
        mesh=mesh,
        in_specs=(
            P(None, None, "ev", None),
            P(None, None, "st", None, "ev"),
            P(None, None, "ev", "st"),
            P("ev", "st"),
        ),
        out_specs=P(None, ("ev", "st")),
        check_vma=False,
    )
```

```python
import jax
import jax.numpy as jnp
from jax import lax
from jax.experimental import pallas as pl
from jax.experimental.pallas import tpu as pltpu
from jax.sharding import PartitionSpec as P

MESH = pl.DeviceIdType.MESH
CORNERS = ((1, 1), (3, 3), (1, 3), (3, 1), (1, 2), (3, 2), (2, 1), (2, 3), (2, 2))
ALONG = ((1, 0), (0, 1), (3, 0), (0, 3), (2, 0), (0, 2))
FAR, NEAR, WHOLE = 0, 1, 2
WHOLE_GROUPS, WHOLE_ALONG = 6, 4


def kernel(strain, green, weights, mask, out, sbuf, wbuf, gs, lhs, held, acc, kbuf, krx, wraw, mraw,
           lsem, s_all, r_w, r_c, r_d, r_f, r_r, r_k):
    ev, st = lax.axis_index("ev"), lax.axis_index("st")
    y, zl, c = ev >> 3, (ev >> 1) & 3, ev & 1
    zh, x = st >> 2, st & 3
    z = zh * 4 + zl
    cores = (c, 1 - c)
    row = [((y + dy) & 3) * 8 for dy in range(4)]
    step_z = {(0, k): 0 for k in (0, 1)} | {(1, k): 1 for k in (0, 1)} | {(3, k): -1 for k in (0, 1)}
    step_z |= {(2, k): 2 - 4 * cores[k] for k in (0, 1)}
    place_to = {at: (z + step) & 7 for at, step in step_z.items()}
    place_from = {dz: (z - step_z[dz, 0]) & 7 for dz in range(4)}
    place_half = [zh * 4 + ((zl + dz) & 3) for dz in range(4)]
    xs = [(x + dx) & 3 for dx in range(4)]

    def device(x_, row_, place, core):
        return (row_ + (place & 3) * 2 + core, (place >> 2) * 4 + x_)

    def lanes(part, half):
        if part == WHOLE:
            return pl.ds(0, 256)
        return pl.ds(pl.multiple_of((1 - half if part == FAR else half) * 128, 128), 128)

    def send(src, dst, send_sem, recv_sem, to):
        pltpu.make_async_remote_copy(
            src_ref=src, dst_ref=dst, send_sem=send_sem, recv_sem=recv_sem,
            device_id=to, device_id_type=MESH).start()

    def arrived(ref, sem):
        pltpu.make_async_remote_copy(
            src_ref=ref, dst_ref=ref, send_sem=s_all.at[0], recv_sem=sem,
            device_id=right, device_id_type=MESH).wait_recv()

    def left(ref, sem):
        pltpu.make_async_remote_copy(
            src_ref=ref, dst_ref=ref, send_sem=sem, recv_sem=r_w.at[0],
            device_id=right, device_id_type=MESH).wait_send()

    right_of, left_of = (ev, zh * 4 + xs[1]), (ev, zh * 4 + xs[3])
    right = right_of
    across = (ev + 1 - 2 * c, st)

    barrier = pltpu.get_barrier_semaphore()
    senders = []
    for dy in (2, 1, 3, 0):
        for dz in (2, 1, 3, 0):
            if dy or dz:
                for core in (0, 1):
                    senders.append(device(x, row[-dy], place_from[dz], core))
    for dz in (1, 2, 3):
        senders.append(device(x, row[0], place_half[4 - dz], c))
    for dx in (1, 3):
        senders.append((ev, zh * 4 + xs[dx]))
    senders.append((ev + 1 - 2 * c, st))
    for d in senders:
        pl.semaphore_signal(barrier, inc=1, device_id=d, device_id_type=MESH)

    load_pair = [
        pltpu.make_async_copy(weights, wraw, lsem.at[7]), pltpu.make_async_copy(mask, mraw, lsem.at[8])]
    for copy in load_pair:
        copy.start()
    load_green = [
        pltpu.make_async_copy(green.at[k], gs.at[:, pl.ds(k * 128, 128), :], lsem.at[1 + k]) for k in range(6)]
    for copy in load_green:
        copy.start()
    own_cells = pl.ds(pl.multiple_of(ev * 256, 256), 256)
    load_own = pltpu.make_async_copy(strain.at[:, :, own_cells], sbuf.at[0, 0, 0], lsem.at[0])
    load_own.start()
    for copy in load_pair:
        copy.wait()
    wbuf[0, 0, 0] = wraw[...] * mraw[...].astype(jnp.bfloat16)[None]
    pl.semaphore_wait(barrier, len(senders))

    for dz in (1, 2, 3):
        send(wbuf.at[0, 0, 0], wbuf.at[0, 0, dz], s_all.at[0], r_w.at[0], device(x, row[0], place_half[dz], c))

    mine = pl.ds(3 * x, 3)
    whole = pl.ds(0, 12)
    both = pl.ds(0, 2)

    def strain_to(dy, dz, dc, slabs, part, send_sem, recv_sem):
        place = place_to[dz, dc]
        to = device(x, row[dy], place, cores[dc])
        at = lanes(part, place >> 2)
        start = pl.multiple_of(to[0] * 256 + at.start, 128)
        send(strain.at[slabs, :, pl.ds(start, at.size)], sbuf.at[dc, dy, dz, slabs, :, at], send_sem, recv_sem, to)

    def parts_of(count, first_split):
        for n in range(first_split):
            yield n, WHOLE
        for part in (FAR, NEAR):
            for n in range(first_split, count):
                yield n, part

    GP = list(parts_of(9, WHOLE_GROUPS))
    DP = list(parts_of(6, WHOLE_ALONG))

    def send_corner(g, part):
        for dc in (0, 1):
            strain_to(*CORNERS[g], dc, mine, part, s_all.at[3], r_c.at[g, part])

    def send_direct(n, part):
        for dc in (0, 1):
            strain_to(*ALONG[n], dc, whole, part, s_all.at[4], r_d.at[n, part])

    strain_to(0, 0, 1, whole, WHOLE, s_all.at[5], r_w.at[3])
    def weights_up():
        arrived(wbuf.at[0, 0, pl.ds(1, 3)], r_w.at[0])
        for dy in (1, 3, 2):
            send(wbuf.at[0, 0], wbuf.at[0, dy], s_all.at[1], r_w.at[1], (row[dy] + (ev & 7), st))

    def block(dcs, g, slabs, part):
        return sbuf.at[dcs, CORNERS[g][0], CORNERS[g][1], slabs, :, lanes(part, zh)]

    def forward(g, part):
        b = block(both, g, mine, part)
        arrived(b, r_c.at[g, part])
        for to in (right_of, left_of):
            send(b, b, s_all.at[6], r_f.at[g, part], to)

    def relay(g, part):
        arrived(block(both, g, pl.ds(0, 6), part), r_f.at[g, part])
        for dc, of_x, to in ((0, xs[3], right_of), (1, xs[1], left_of)):
            b = block(dc, g, pl.ds(3 * of_x, 3), part)
            send(b, b, s_all.at[7], r_r.at[g, part], to)

    def weights_across():
        arrived(wbuf.at[0, pl.ds(1, 3)], r_w.at[1])
        send(wbuf.at[0], wbuf.at[1], s_all.at[2], r_w.at[2], across)

    def left_side():
        arrived(wbuf.at[1], r_w.at[2])
        all_w = wbuf.reshape(32, 6, 16, 128)
        for f in range(3):
            real = all_w[:, f].reshape(512, 128)
            imag = all_w[:, 3 + f].reshape(512, 128)
            lhs[0:512, f * 128:(f + 1) * 128] = real
            lhs[0:512, 384 + f * 128:384 + (f + 1) * 128] = -imag
            lhs[512:1024, f * 128:(f + 1) * 128] = imag
            lhs[512:1024, 384 + f * 128:384 + (f + 1) * 128] = real
        for copy in load_green:
            copy.wait()

    def multiply(v, _):
        held[v] = jnp.dot(lhs[...], gs[v], preferred_element_type=jnp.float32)
        return 0

    def products(first, last):
        lax.fori_loop(first, last, multiply, 0)

    acc[...] = jnp.zeros_like(acc)

    def add_up(slot, part):
        dc, dy, dz = slot
        first = (dc * 16 + dy * 4 + dz) * 16
        at = lanes(part, zh)
        s = sbuf[dc, dy, dz, :, :, at].astype(jnp.float32)
        hr = [held[v, pl.ds(first, 16), at] for v in range(6)]
        hi = [held[v, pl.ds(512 + first, 16), at] for v in range(6)]
        trace = (s[0] + s[1] + s[2]) * (hr[0] + hr[1] + hr[2]) - (s[6] + s[7] + s[8]) * (hi[0] + hi[1] + hi[2])
        normal = sum(s[v] * hr[v] - s[6 + v] * hi[v] for v in range(3))
        shear = sum(s[v] * hr[v] - s[6 + v] * hi[v] for v in range(3, 6))
        acc[0, :, at] += trace
        acc[1, :, at] += normal + 2.0 * shear

    def take_direct(n, part):
        arrived(sbuf.at[both, ALONG[n][0], ALONG[n][1], :, :, lanes(part, zh)], r_d.at[n, part])
        for dc in (0, 1):
            add_up((dc, *ALONG[n]), part)

    def take_corner(g, part):
        arrived(block(both, g, pl.ds(0, 3), part), r_r.at[g, part])
        for dc in (0, 1):
            add_up((dc, *CORNERS[g]), part)

    def share(dh):
        kbuf[dh, 0:2] = acc[:, :, lanes(NEAR if dh == 0 else FAR, zh)].sum(axis=1)
        for dx in (2, 1, 3, 0):
            if dx or dh:
                send(kbuf.at[dh], krx.at[4 * dh + dx], s_all.at[8 + dh], r_k.at[dh], (ev, (zh ^ dh) * 4 + xs[dx]))

    for stage in GP[0:12]:
        send_corner(*stage)
    weights_up()
    for stage in DP[0:8]:
        send_direct(*stage)
    for stage in GP[0:12]:
        forward(*stage)
    for stage in GP[0:5]:
        relay(*stage)
    weights_across()
    for stage in GP[5:8]:
        relay(*stage)
    left_side()
    products(0, 3)
    relay(*GP[8])
    products(3, 6)
    load_own.wait()
    add_up((0, 0, 0), WHOLE)
    arrived(sbuf.at[1, 0, 0], r_w.at[3])
    add_up((1, 0, 0), WHOLE)
    for stage in DP[0:4]:
        take_direct(*stage)
    for stage in GP[9:12]:
        relay(*stage)
    for stage in GP[0:6]:
        take_corner(*stage)
    for stage in DP[4:6]:
        take_direct(*stage)
    for stage in GP[6:9]:
        take_corner(*stage)
    share(1)
    for stage in DP[6:8]:
        take_direct(*stage)
    for stage in GP[9:12]:
        take_corner(*stage)
    share(0)
    left(wbuf.at[0, 0, pl.ds(1, 3)], s_all.at[0])
    left(wbuf.at[0, pl.ds(1, 3)], s_all.at[1])
    left(wbuf.at[0], s_all.at[2])
    left(sbuf.at[0, pl.ds(0, 3), pl.ds(0, 3), pl.ds(0, 6)], s_all.at[3])
    left(sbuf.at[0, pl.ds(0, 3)], s_all.at[4])
    left(sbuf.at[0, 0, 0], s_all.at[5])
    left(sbuf.at[0, pl.ds(0, 3), pl.ds(0, 3)], s_all.at[6])
    left(sbuf.at[0, pl.ds(0, 3), pl.ds(0, 3), pl.ds(0, 6)], s_all.at[7])
    arrived(krx.at[pl.ds(4, 4)], r_k.at[1])
    other = krx[4] + krx[5] + krx[6] + krx[7]
    arrived(krx.at[pl.ds(1, 3)], r_k.at[0])
    same = kbuf[0] + krx[1] + krx[2] + krx[3]

    def own_cells_of(total):
        result = total[0:2, 0:32]
        for k in range(1, 4):
            result = jnp.where(x == k, total[0:2, 32 * k:32 * k + 32], result)
        return result

    out[0] = own_cells_of(same)
    out[1] = own_cells_of(other)
    left(krx.at[pl.ds(1, 3)], s_all.at[8])
    left(krx.at[pl.ds(4, 4)], s_all.at[9])


def local(strain, green, weights, mask):
    sums = pl.pallas_call(
        kernel,
        out_shape=pltpu.VMEM((2, 2, 32), jnp.float32),
        in_specs=[
            pl.BlockSpec(memory_space=pl.ANY),
            pl.BlockSpec(memory_space=pl.ANY),
            pl.BlockSpec(memory_space=pl.ANY),
            pl.BlockSpec(memory_space=pl.ANY),
        ],
        out_specs=pl.BlockSpec(memory_space=pltpu.VMEM),
        scratch_shapes=[
            pltpu.VMEM((2, 4, 4, 12, 16, 256), jnp.bfloat16),
            pltpu.VMEM((2, 4, 4, 6, 16, 128), jnp.bfloat16),
            pltpu.VMEM((6, 768, 256), jnp.bfloat16),
            pltpu.VMEM((1024, 768), jnp.bfloat16),
            pltpu.VMEM((6, 1024, 256), jnp.float32),
            pltpu.VMEM((2, 16, 256), jnp.float32),
            pltpu.VMEM((2, 8, 128), jnp.float32),
            pltpu.VMEM((8, 8, 128), jnp.float32),
            pltpu.VMEM((6, 16, 128), jnp.bfloat16),
            pltpu.VMEM((16, 128), jnp.int32),
            pltpu.SemaphoreType.DMA((9,)),
            pltpu.SemaphoreType.DMA((10,)),
            pltpu.SemaphoreType.DMA((4,)),
            pltpu.SemaphoreType.DMA((9, 3)),
            pltpu.SemaphoreType.DMA((6, 3)),
            pltpu.SemaphoreType.DMA((9, 3)),
            pltpu.SemaphoreType.DMA((9, 3)),
            pltpu.SemaphoreType.DMA((2,)),
        ],
        compiler_params=pltpu.CompilerParams(
            collective_id=0, has_side_effects=True, vmem_limit_bytes=60 << 20),
    )(strain.reshape(12, *strain.shape[2:]), jnp.swapaxes(green, 2, 3).reshape(6, 6, 128, 256),
      weights.reshape(6, *weights.shape[2:]), mask)
    return sums[0] + sums[1]


def solution(mesh):
    return jax.shard_map(
        local,
        mesh=mesh,
        in_specs=(
            P(None, None, "ev", None),
            P(None, None, "st", None, "ev"),
            P(None, None, "ev", "st"),
            P("ev", "st"),
        ),
        out_specs=P(None, ("ev", "st")),
        check_vma=False,
    )
```

```python
import jax
import jax.numpy as jnp
from jax import lax
from jax.experimental import pallas as pl
from jax.experimental.pallas import tpu as pltpu
from jax.sharding import PartitionSpec as P

MESH = pl.DeviceIdType.MESH
CORNERS = ((1, 1), (3, 3), (1, 3), (3, 1), (1, 2), (3, 2), (2, 1), (2, 3), (2, 2))
ALONG = ((1, 0), (0, 1), (3, 0), (0, 3), (2, 0), (0, 2))
FAR, NEAR, WHOLE = 0, 1, 2
WHOLE_GROUPS, WHOLE_ALONG = 6, 2


def kernel(strain, green, weights, mask, out, sbuf, wbuf, gs, lhs, held, acc, kbuf, krx, wraw, mraw,
           lsem, s_all, r_w, r_c, r_d, r_f, r_r, r_k):
    ev, st = lax.axis_index("ev"), lax.axis_index("st")
    y, zl, c = ev >> 3, (ev >> 1) & 3, ev & 1
    zh, x = st >> 2, st & 3
    z = zh * 4 + zl
    cores = (c, 1 - c)
    row = [((y + dy) & 3) * 8 for dy in range(4)]
    step_z = {(0, k): 0 for k in (0, 1)} | {(1, k): 1 for k in (0, 1)} | {(3, k): -1 for k in (0, 1)}
    step_z |= {(2, k): 2 - 4 * cores[k] for k in (0, 1)}
    place_to = {at: (z + step) & 7 for at, step in step_z.items()}
    place_from = {dz: (z - step_z[dz, 0]) & 7 for dz in range(4)}
    place_half = [zh * 4 + ((zl + dz) & 3) for dz in range(4)]
    xs = [(x + dx) & 3 for dx in range(4)]

    def device(x_, row_, place, core):
        return (row_ + (place & 3) * 2 + core, (place >> 2) * 4 + x_)

    def lanes(part, half):
        if part == WHOLE:
            return pl.ds(0, 256)
        return pl.ds(pl.multiple_of((1 - half if part == FAR else half) * 128, 128), 128)

    def send(src, dst, send_sem, recv_sem, to):
        pltpu.make_async_remote_copy(
            src_ref=src, dst_ref=dst, send_sem=send_sem, recv_sem=recv_sem,
            device_id=to, device_id_type=MESH).start()

    def arrived(ref, sem):
        pltpu.make_async_remote_copy(
            src_ref=ref, dst_ref=ref, send_sem=s_all.at[0], recv_sem=sem,
            device_id=right, device_id_type=MESH).wait_recv()

    def left(ref, sem):
        pltpu.make_async_remote_copy(
            src_ref=ref, dst_ref=ref, send_sem=sem, recv_sem=r_w.at[0],
            device_id=right, device_id_type=MESH).wait_send()

    right_of, left_of = (ev, zh * 4 + xs[1]), (ev, zh * 4 + xs[3])
    right = right_of
    across = (ev + 1 - 2 * c, st)

    barrier = pltpu.get_barrier_semaphore()
    senders = []
    for dy in (2, 1, 3, 0):
        for dz in (2, 1, 3, 0):
            if dy or dz:
                for core in (0, 1):
                    senders.append(device(x, row[-dy], place_from[dz], core))
    for dz in (1, 2, 3):
        senders.append(device(x, row[0], place_half[4 - dz], c))
    for dx in (1, 3):
        senders.append((ev, zh * 4 + xs[dx]))
    senders.append((ev + 1 - 2 * c, st))
    for d in senders:
        pl.semaphore_signal(barrier, inc=1, device_id=d, device_id_type=MESH)

    load_pair = [
        pltpu.make_async_copy(weights, wraw, lsem.at[7]), pltpu.make_async_copy(mask, mraw, lsem.at[8])]
    for copy in load_pair:
        copy.start()
    load_green = [
        pltpu.make_async_copy(green.at[k], gs.at[:, pl.ds(k * 128, 128), :], lsem.at[1 + k]) for k in range(6)]
    for copy in load_green:
        copy.start()
    own_cells = pl.ds(pl.multiple_of(ev * 256, 256), 256)
    load_own = pltpu.make_async_copy(strain.at[:, :, own_cells], sbuf.at[0, 0, 0], lsem.at[0])
    load_own.start()
    for copy in load_pair:
        copy.wait()
    wbuf[0, 0, 0] = wraw[...] * mraw[...].astype(jnp.bfloat16)[None]
    pl.semaphore_wait(barrier, len(senders))

    for dz in (1, 2, 3):
        send(wbuf.at[0, 0, 0], wbuf.at[0, 0, dz], s_all.at[0], r_w.at[0], device(x, row[0], place_half[dz], c))

    mine = pl.ds(3 * x, 3)
    whole = pl.ds(0, 12)
    both = pl.ds(0, 2)

    def strain_to(dy, dz, dc, slabs, part, send_sem, recv_sem):
        place = place_to[dz, dc]
        to = device(x, row[dy], place, cores[dc])
        at = lanes(part, place >> 2)
        start = pl.multiple_of(to[0] * 256 + at.start, 128)
        send(strain.at[slabs, :, pl.ds(start, at.size)], sbuf.at[dc, dy, dz, slabs, :, at], send_sem, recv_sem, to)

    def parts_of(count, first_split):
        for n in range(first_split):
            yield n, WHOLE
        for part in (FAR, NEAR):
            for n in range(first_split, count):
                yield n, part

    GP = list(parts_of(9, WHOLE_GROUPS))
    DP = list(parts_of(6, WHOLE_ALONG))

    def send_corner(g, part):
        for dc in (0, 1):
            strain_to(*CORNERS[g], dc, mine, part, s_all.at[3], r_c.at[g, part])

    def send_direct(n, part):
        for dc in (0, 1):
            strain_to(*ALONG[n], dc, whole, part, s_all.at[4], r_d.at[n, part])

    strain_to(0, 0, 1, whole, WHOLE, s_all.at[5], r_w.at[3])
    def weights_up():
        arrived(wbuf.at[0, 0, pl.ds(1, 3)], r_w.at[0])
        for dy in (1, 3, 2):
            send(wbuf.at[0, 0], wbuf.at[0, dy], s_all.at[1], r_w.at[1], (row[dy] + (ev & 7), st))

    def block(dcs, g, slabs, part):
        return sbuf.at[dcs, CORNERS[g][0], CORNERS[g][1], slabs, :, lanes(part, zh)]

    def forward(g, part):
        b = block(both, g, mine, part)
        arrived(b, r_c.at[g, part])
        for to in (right_of, left_of):
            send(b, b, s_all.at[6], r_f.at[g, part], to)

    def relay(g, part):
        arrived(block(both, g, pl.ds(0, 6), part), r_f.at[g, part])
        for dc, of_x, to in ((0, xs[3], right_of), (1, xs[1], left_of)):
            b = block(dc, g, pl.ds(3 * of_x, 3), part)
            send(b, b, s_all.at[7], r_r.at[g, part], to)

    def weights_across():
        arrived(wbuf.at[0, pl.ds(1, 3)], r_w.at[1])
        send(wbuf.at[0], wbuf.at[1], s_all.at[2], r_w.at[2], across)

    def left_side():
        arrived(wbuf.at[1], r_w.at[2])
        all_w = wbuf.reshape(32, 6, 16, 128)
        for f in range(3):
            real = all_w[:, f].reshape(512, 128)
            imag = all_w[:, 3 + f].reshape(512, 128)
            lhs[0:512, f * 128:(f + 1) * 128] = real
            lhs[0:512, 384 + f * 128:384 + (f + 1) * 128] = -imag
            lhs[512:1024, f * 128:(f + 1) * 128] = imag
            lhs[512:1024, 384 + f * 128:384 + (f + 1) * 128] = real
        for copy in load_green:
            copy.wait()

    def multiply(v, _):
        held[v] = jnp.dot(lhs[...], gs[v], preferred_element_type=jnp.float32)
        return 0

    def products(first, last):
        lax.fori_loop(first, last, multiply, 0)

    acc[...] = jnp.zeros_like(acc)

    def add_up(slot, part):
        dc, dy, dz = slot
        first = (dc * 16 + dy * 4 + dz) * 16
        at = lanes(part, zh)
        s = sbuf[dc, dy, dz, :, :, at].astype(jnp.float32)
        hr = [held[v, pl.ds(first, 16), at] for v in range(6)]
        hi = [held[v, pl.ds(512 + first, 16), at] for v in range(6)]
        trace = (s[0] + s[1] + s[2]) * (hr[0] + hr[1] + hr[2]) - (s[6] + s[7] + s[8]) * (hi[0] + hi[1] + hi[2])
        normal = sum(s[v] * hr[v] - s[6 + v] * hi[v] for v in range(3))
        shear = sum(s[v] * hr[v] - s[6 + v] * hi[v] for v in range(3, 6))
        acc[0, :, at] += trace
        acc[1, :, at] += normal + 2.0 * shear

    def take_direct(n, part):
        arrived(sbuf.at[both, ALONG[n][0], ALONG[n][1], :, :, lanes(part, zh)], r_d.at[n, part])
        for dc in (0, 1):
            add_up((dc, *ALONG[n]), part)

    def take_corner(g, part):
        arrived(block(both, g, pl.ds(0, 3), part), r_r.at[g, part])
        for dc in (0, 1):
            add_up((dc, *CORNERS[g]), part)

    def share(dh):
        kbuf[dh, 0:2] = acc[:, :, lanes(NEAR if dh == 0 else FAR, zh)].sum(axis=1)
        for dx in (2, 1, 3, 0):
            if dx or dh:
                send(kbuf.at[dh], krx.at[4 * dh + dx], s_all.at[8 + dh], r_k.at[dh], (ev, (zh ^ dh) * 4 + xs[dx]))

    for stage in GP[0:12]:
        send_corner(*stage)
    weights_up()
    for stage in DP[0:10]:
        send_direct(*stage)
    for stage in GP[0:12]:
        forward(*stage)
    for stage in GP[0:5]:
        relay(*stage)
    weights_across()
    for stage in GP[5:8]:
        relay(*stage)
    left_side()
    products(0, 3)
    relay(*GP[8])
    products(3, 6)
    load_own.wait()
    add_up((0, 0, 0), WHOLE)
    arrived(sbuf.at[1, 0, 0], r_w.at[3])
    add_up((1, 0, 0), WHOLE)
    for stage in DP[0:2]:
        take_direct(*stage)
    for stage in GP[9:12]:
        relay(*stage)
    for stage in GP[0:6]:
        take_corner(*stage)
    for stage in DP[2:6]:
        take_direct(*stage)
    for stage in GP[6:9]:
        take_corner(*stage)
    share(1)
    for stage in DP[6:10]:
        take_direct(*stage)
    for stage in GP[9:12]:
        take_corner(*stage)
    share(0)
    left(wbuf.at[0, 0, pl.ds(1, 3)], s_all.at[0])
    left(wbuf.at[0, pl.ds(1, 3)], s_all.at[1])
    left(wbuf.at[0], s_all.at[2])
    left(sbuf.at[0, pl.ds(0, 3), pl.ds(0, 3), pl.ds(0, 6)], s_all.at[3])
    left(sbuf.at[0, pl.ds(0, 3)], s_all.at[4])
    left(sbuf.at[0, 0, 0], s_all.at[5])
    left(sbuf.at[0, pl.ds(0, 3), pl.ds(0, 3)], s_all.at[6])
    left(sbuf.at[0, pl.ds(0, 3), pl.ds(0, 3), pl.ds(0, 6)], s_all.at[7])
    arrived(krx.at[pl.ds(4, 4)], r_k.at[1])
    other = krx[4] + krx[5] + krx[6] + krx[7]
    arrived(krx.at[pl.ds(1, 3)], r_k.at[0])
    same = kbuf[0] + krx[1] + krx[2] + krx[3]

    def own_cells_of(total):
        result = total[0:2, 0:32]
        for k in range(1, 4):
            result = jnp.where(x == k, total[0:2, 32 * k:32 * k + 32], result)
        return result

    out[0] = own_cells_of(same)
    out[1] = own_cells_of(other)
    left(krx.at[pl.ds(1, 3)], s_all.at[8])
    left(krx.at[pl.ds(4, 4)], s_all.at[9])


def local(strain, green, weights, mask):
    sums = pl.pallas_call(
        kernel,
        out_shape=pltpu.VMEM((2, 2, 32), jnp.float32),
        in_specs=[
            pl.BlockSpec(memory_space=pl.ANY),
            pl.BlockSpec(memory_space=pl.ANY),
            pl.BlockSpec(memory_space=pl.ANY),
            pl.BlockSpec(memory_space=pl.ANY),
        ],
        out_specs=pl.BlockSpec(memory_space=pltpu.VMEM),
        scratch_shapes=[
            pltpu.VMEM((2, 4, 4, 12, 16, 256), jnp.bfloat16),
            pltpu.VMEM((2, 4, 4, 6, 16, 128), jnp.bfloat16),
            pltpu.VMEM((6, 768, 256), jnp.bfloat16),
            pltpu.VMEM((1024, 768), jnp.bfloat16),
            pltpu.VMEM((6, 1024, 256), jnp.float32),
            pltpu.VMEM((2, 16, 256), jnp.float32),
            pltpu.VMEM((2, 8, 128), jnp.float32),
            pltpu.VMEM((8, 8, 128), jnp.float32),
            pltpu.VMEM((6, 16, 128), jnp.bfloat16),
            pltpu.VMEM((16, 128), jnp.int32),
            pltpu.SemaphoreType.DMA((9,)),
            pltpu.SemaphoreType.DMA((10,)),
            pltpu.SemaphoreType.DMA((4,)),
            pltpu.SemaphoreType.DMA((9, 3)),
            pltpu.SemaphoreType.DMA((6, 3)),
            pltpu.SemaphoreType.DMA((9, 3)),
            pltpu.SemaphoreType.DMA((9, 3)),
            pltpu.SemaphoreType.DMA((2,)),
        ],
        compiler_params=pltpu.CompilerParams(
            collective_id=0, has_side_effects=True, vmem_limit_bytes=60 << 20),
    )(strain.reshape(12, *strain.shape[2:]), jnp.swapaxes(green, 2, 3).reshape(6, 6, 128, 256),
      weights.reshape(6, *weights.shape[2:]), mask)
    return sums[0] + sums[1]


def solution(mesh):
    return jax.shard_map(
        local,
        mesh=mesh,
        in_specs=(
            P(None, None, "ev", None),
            P(None, None, "st", None, "ev"),
            P(None, None, "ev", "st"),
            P("ev", "st"),
        ),
        out_specs=P(None, ("ev", "st")),
        check_vma=False,
    )
```
